256 devices in a mesh: row: 32 (over y, x, core), col: 8 (over z).
Axes of the slice: x: 4, y: 4, z: 8, core: 2. Of those that a mesh axis runs over, the one named last changes fastest.
Arguments:
- activations: bfloat16 [512, 12288], P('row', 'col'), may hold values from -6 to 6
- w_in: bfloat16 [12288, 24576], P('col', 'row'), may hold values from -0.0546875 to 0.0546875
- bias_in: float32 [24576], P('row'), may hold values from -5 to 5
- w_out: bfloat16 [24576, 12288], P('row', 'col'), may hold values from -0.0390625 to 0.0390625
- cotangent: bfloat16 [512, 12288], P('row', 'col'), may hold values from -6 to 6
Outputs:
- outputs: bfloat16 [512, 12288], P('row', 'col')
- input_grad: bfloat16 [512, 12288], P('row', 'col')
- w_in_grad: bfloat16 [12288, 24576], P('col', 'row')
- w_out_grad: bfloat16 [24576, 12288], P('row', 'col')
- bias_grad: float32 [24576], P('row')
The draws below stay inside these ranges and needn't reach their ends.
All inputs are finite; a program needn't handle non-finite values.
Results may differ from the reference program's by a relative error of at most 0.005.
Values may be sent and summed in bfloat16 or wider, within the bound.
No kernel may reach another device: no remote copies, remote signals or barrier semaphores. Data moves between devices by JAX's collectives and lax.ppermute only.
A program may use at most 64 MiB of HBM per device.

```python
import math
import jax
import jax.numpy as jnp
from jax import lax

D = 12288
FF = 24576
TOKENS = 512


def steps_of(key, extent, pieces, low, top_value):
    def one(axis_at, blocks):
        steps = jax.random.uniform(jax.random.fold_in(jax.random.fold_in(key, 6), axis_at), (blocks,), jnp.float32, low / len(pieces), top_value / len(pieces))
        return jnp.repeat(jnp.exp(steps), extent[axis_at] // blocks).reshape((-1,) + (1,) * (len(extent) - axis_at - 1))

    factor_of = one(*pieces[0])
    for cut in pieces[1:]:
        factor_of = factor_of * one(*cut)
    return factor_of


def gaussian(key, dims, spread, limit, cuts=(), held_as=jnp.bfloat16):
    result = spread * jax.random.normal(key, dims, jnp.float32)
    if cuts:
        result = result * steps_of(key, dims, cuts, -0.22, 0.18)
    return jnp.clip(result, -limit, limit).astype(held_as)


def setup_inputs(seed: int = 0) -> dict:
    streams_of = jax.random.split(jax.random.key(seed), 6)
    return {
        "activations": gaussian(streams_of[0], (TOKENS, D), 1.0, 6.0, ((0, 32), (1, 8))),
        "w_in": gaussian(streams_of[1], (D, FF), D ** -0.5, 0.0546875, ((0, 8), (1, 32))),
        "bias_in": gaussian(streams_of[2], (FF,), 1.0, 5.0, ((0, 32),), jnp.float32),
        "w_out": gaussian(streams_of[3], (FF, D), FF ** -0.5, 0.0390625, ((0, 32), (1, 8))),
        "cotangent": gaussian(streams_of[4], (TOKENS, D), 1.0, 6.0, ((0, 32), (1, 8))),
    }


root_coef = math.sqrt(2.0 / math.pi)

def gelu_tanh(values):
    inner = root_coef * (values + 0.044715 * values * values * values)
    return 0.5 * values * (1.0 + jnp.tanh(inner))

def gelu_slope(values):
    inner = root_coef * (values + 0.044715 * values * values * values)
    tanh_val = jnp.tanh(inner)
    return 0.5 * (1.0 + tanh_val) + 0.5 * values * (1.0 - tanh_val * tanh_val) * root_coef * (1.0 + 3.0 * 0.044715 * values * values)

def reference(activations, w_in, bias_in, w_out, cotangent):
    pre_act = jnp.dot(activations, w_in, preferred_element_type=jnp.float32) + bias_in
    hidden = gelu_tanh(pre_act).astype(jnp.bfloat16)
    outputs = jnp.dot(hidden, w_out, preferred_element_type=jnp.float32).astype(jnp.bfloat16)
    hidden_grad = lax.dot_general(cotangent, w_out, (((1,), (1,)), ((), ())), preferred_element_type=jnp.float32)
    pre_grad = hidden_grad * gelu_slope(pre_act)
    pre_grad_b = pre_grad.astype(jnp.bfloat16)
    grad_scale = jnp.float32(1.0 / math.sqrt(TOKENS))
    bias_grad = lax.optimization_barrier(jnp.sum(pre_grad, axis=0)) * grad_scale
    w_in_grad = (lax.dot_general(activations, pre_grad_b, (((0,), (0,)), ((), ())), preferred_element_type=jnp.float32) * grad_scale).astype(jnp.bfloat16)
    w_out_grad = (lax.dot_general(hidden, cotangent, (((0,), (0,)), ((), ())), preferred_element_type=jnp.float32) * grad_scale).astype(jnp.bfloat16)
    input_grad = lax.dot_general(pre_grad_b, w_in, (((1,), (1,)), ((), ())), preferred_element_type=jnp.float32).astype(jnp.bfloat16)
    return (outputs, input_grad, w_in_grad, w_out_grad, bias_grad)
```

```python
import math

import jax
import jax.numpy as jnp
from jax import lax
from jax.sharding import PartitionSpec as P

TOKENS = 512
HALF = 256
BF16 = jnp.bfloat16
F32 = jnp.float32

root_coef = math.sqrt(2.0 / math.pi)


def gelu_and_slope(values):
    inner = root_coef * (values + 0.044715 * values * values * values)
    tanh_val = jnp.tanh(inner)
    gelu = 0.5 * values * (1.0 + tanh_val)
    slope = 0.5 * (1.0 + tanh_val) + 0.5 * values * (1.0 - tanh_val * tanh_val) * root_coef * (
        1.0 + 3.0 * 0.044715 * values * values
    )
    return gelu, slope


def matmul(left, right):
    return jnp.dot(left, right, preferred_element_type=F32)


def contract_rows(left, right):
    return lax.dot_general(
        left, right, (((0,), (0,)), ((), ())), preferred_element_type=F32
    )


def contract_cols(left, right):
    return lax.dot_general(
        left, right, (((1,), (1,)), ((), ())), preferred_element_type=F32
    )


def row_of(y, x, core):
    return (y * 4 + x) * 2 + core


def ring_partner(at, size, odd_links):
    return (at + 1) % size if (at % 2 == 1) == odd_links else (at - 1) % size


def plane_swap(values, kind, first):
    pairs = []
    for y in range(4):
        for x in range(4):
            for core in range(2):
                along_x = (core == 0) == first
                at = x if along_x else y
                to = (at + 2) % 4 if kind == 2 else ring_partner(at, 4, kind == 3)
                pairs.append((row_of(y, x, core), row_of(y, to, core) if along_x else row_of(to, x, core)))
    return lax.ppermute(values, "row", pairs)


def swap_cores(values):
    return lax.ppermute(values, "row", [(i, i ^ 1) for i in range(32)])


def col_swap(values, odd_links):
    return lax.ppermute(values, "col", [(i, ring_partner(i, 8, odd_links)) for i in range(8)])


def local(activations, w_in, bias_in, w_out, cotangent):
    grad_scale = jnp.float32(1.0 / math.sqrt(TOKENS))
    features = activations.shape[1]
    hidden_here = w_in.shape[1]
    me = lax.axis_index("col")
    way = 1 - 2 * (me % 2)

    mine = jnp.stack([activations, cotangent])
    got = {k: plane_swap(mine, k, True) for k in (2, 1, 3)}
    line = jnp.stack([mine, got[1], got[2], got[3]], axis=1)
    got = {k: plane_swap(line, k, False) for k in (2, 1, 3)}
    own = jnp.stack([line, got[1], got[2], got[3]], axis=1).reshape(2, HALF, features)
    other = swap_cores(own)

    def first_products(tokens):
        return matmul(tokens[0], w_in), contract_cols(tokens[1], w_out)

    own_parts = first_products(own)

    def part(halves, j):
        at = ((me + way * j) % 8) * 32
        return jnp.stack(
            [jnp.stack([lax.dynamic_slice_in_dim(x, at, 32, 0) for x in half]) for half in halves]
        )

    far_own = part([own_parts], 4).astype(BF16)
    far_own, other = lax.optimization_barrier((far_own, other))
    from_even = col_swap(far_own, False)
    other_parts = first_products(other)
    from_odd = col_swap(part([other_parts], 4).astype(BF16), True)
    halves = [own_parts, other_parts]
    to_odd = jnp.concatenate([part([own_parts], -3) + from_even.astype(F32), part([other_parts], -3)])
    to_even = jnp.concatenate([part([own_parts], 3), part([other_parts], 3) + from_odd.astype(F32)])
    for j in (2, 1):
        from_odd = col_swap(to_odd.astype(BF16), True)
        from_even = col_swap(to_even.astype(BF16), False)
        to_odd = part(halves, -j) + from_even.astype(F32)
        to_even = part(halves, j) + from_odd.astype(F32)
    from_odd = col_swap(to_odd.astype(BF16), True)
    from_even = col_swap(to_even.astype(BF16), False)
    total = part(halves, 0) + from_even.astype(F32) + from_odd.astype(F32)

    hidden_mine, slope = gelu_and_slope(total[:, 0] + bias_in)
    both = jnp.stack([hidden_mine.astype(BF16), (total[:, 1] * slope).astype(BF16)], axis=1)

    everything = jnp.zeros((2, 2, 8, 32, hidden_here), BF16)
    evens, odds = [both], [both]
    for _ in range(3):
        from_even, from_odd = col_swap(odds[-1], False), col_swap(evens[-1], True)
        evens.append(from_even)
        odds.append(from_odd)
    opposite = jnp.concatenate([col_swap(odds[3][:1], False), col_swap(evens[3][1:], True)])
    for j, block in enumerate(evens + [opposite] + odds[:0:-1]):
        everything = lax.dynamic_update_slice_in_dim(everything, block[:, :, None], (me + way * j) % 8, 2)
    everything = everything.reshape(2, 2, HALF, hidden_here)

    came_out = swap_cores(matmul(everything[1, 0], w_out).astype(BF16))
    came_grad = swap_cores(contract_cols(everything[1, 1], w_in).astype(BF16))
    kept_out = matmul(everything[0, 0], w_out) + came_out.astype(F32)
    kept_grad = contract_cols(everything[0, 1], w_in) + came_grad.astype(F32)
    kept = [
        jnp.stack([x.reshape(4, 4, 16, features)[k] for x in (kept_out, kept_grad)]) for k in range(4)
    ]
    sent = [x.astype(BF16) for x in kept[1:]]
    everything, own, other, *sent = lax.optimization_barrier((everything, own, other, *sent))
    came = {k: plane_swap(sent[k - 1], k, False) for k in (2, 1, 3)}
    plane_sum = kept[0]
    for k in (1, 2, 3):
        plane_sum = plane_sum + came[k].astype(F32)
    came = {k: plane_swap(plane_sum[:, k].astype(BF16), k, True) for k in (2, 1, 3)}
    line_sum = plane_sum[:, 0]
    for k in (1, 2, 3):
        line_sum = line_sum + came[k].astype(F32)
    result = line_sum.astype(BF16)

    hidden = everything[:, 0].reshape(TOKENS, hidden_here)
    pre_grad = everything[:, 1].reshape(TOKENS, hidden_here)
    all_inputs = jnp.concatenate([own[0], other[0]])
    all_grads = jnp.concatenate([own[1], other[1]])
    bias_grad = jnp.sum(pre_grad.astype(F32), axis=0) * grad_scale
    w_out_grad = (contract_rows(hidden, all_grads) * grad_scale).astype(BF16)
    w_in_grad = (contract_rows(all_inputs, pre_grad) * grad_scale).astype(BF16)
    return (result[0], result[1], w_in_grad, w_out_grad, bias_grad)


def solution(mesh):
    placed = (P("row", "col"), P("col", "row"), P("row"), P("row", "col"), P("row", "col"))
    return jax.shard_map(
        local,
        mesh=mesh,
        in_specs=placed,
        out_specs=(P("row", "col"), P("row", "col"), P("col", "row"), P("row", "col"), P("row")),
        check_vma=False,
    )
```

```python
import math

import jax
import jax.numpy as jnp
from jax import lax
from jax.sharding import PartitionSpec as P

TOKENS = 512
HALF = 256
BF16 = jnp.bfloat16
F32 = jnp.float32

root_coef = math.sqrt(2.0 / math.pi)


def gelu_and_slope(values):
    inner = root_coef * (values + 0.044715 * values * values * values)
    tanh_val = jnp.tanh(inner)
    gelu = 0.5 * values * (1.0 + tanh_val)
    slope = 0.5 * (1.0 + tanh_val) + 0.5 * values * (1.0 - tanh_val * tanh_val) * root_coef * (
        1.0 + 3.0 * 0.044715 * values * values
    )
    return gelu, slope


def matmul(left, right):
    return jnp.dot(left, right, preferred_element_type=F32)


def contract_rows(left, right):
    return lax.dot_general(
        left, right, (((0,), (0,)), ((), ())), preferred_element_type=F32
    )


def contract_cols(left, right):
    return lax.dot_general(
        left, right, (((1,), (1,)), ((), ())), preferred_element_type=F32
    )


def row_of(y, x, core):
    return (y * 4 + x) * 2 + core


def ring_partner(at, size, odd_links):
    return (at + 1) % size if (at % 2 == 1) == odd_links else (at - 1) % size


def plane_swap(values, kind, first):
    pairs = []
    for y in range(4):
        for x in range(4):
            for core in range(2):
                along_x = (core == 0) == first
                at = x if along_x else y
                to = (at + 2) % 4 if kind == 2 else ring_partner(at, 4, kind == 3)
                pairs.append((row_of(y, x, core), row_of(y, to, core) if along_x else row_of(to, x, core)))
    return lax.ppermute(values, "row", pairs)


def swap_cores(values):
    return lax.ppermute(values, "row", [(i, i ^ 1) for i in range(32)])


def col_swap(values, odd_links):
    return lax.ppermute(values, "col", [(i, ring_partner(i, 8, odd_links)) for i in range(8)])


def local(activations, w_in, bias_in, w_out, cotangent):
    grad_scale = jnp.float32(1.0 / math.sqrt(TOKENS))
    features = activations.shape[1]
    hidden_here = w_in.shape[1]
    me = lax.axis_index("col")
    way = 1 - 2 * (me % 2)

    mine = jnp.stack([activations, cotangent])
    got = {k: plane_swap(mine, k, True) for k in (2, 1, 3)}
    line = lax.optimization_barrier(jnp.stack([mine, got[1], got[2], got[3]], axis=1))
    got = {k: plane_swap(line, k, False) for k in (2, 1, 3)}
    own = jnp.stack([line, got[1], got[2], got[3]], axis=1).reshape(2, HALF, features)
    other = swap_cores(own)

    def first_products(tokens):
        return matmul(tokens[0], w_in), contract_cols(tokens[1], w_out)

    own_parts = first_products(own)

    def part(halves, j):
        at = ((me + way * j) % 8) * 32
        return jnp.stack(
            [jnp.stack([lax.dynamic_slice_in_dim(x, at, 32, 0) for x in half]) for half in halves]
        )

    far_own = part([own_parts], 4).astype(BF16)
    far_own, other = lax.optimization_barrier((far_own, other))
    from_even = col_swap(far_own, False)
    other_parts = first_products(other)
    from_odd = col_swap(part([other_parts], 4).astype(BF16), True)
    halves = [own_parts, other_parts]
    from_even, own, other = lax.optimization_barrier((from_even, own, other))
    all_inputs = jnp.concatenate([own[0], other[0]])
    all_grads = jnp.concatenate([own[1], other[1]])
    to_odd = jnp.concatenate([part([own_parts], -3) + from_even.astype(F32), part([other_parts], -3)])
    to_even = jnp.concatenate([part([own_parts], 3), part([other_parts], 3) + from_odd.astype(F32)])
    for j in (2, 1):
        from_odd = col_swap(to_odd.astype(BF16), True)
        from_even = col_swap(to_even.astype(BF16), False)
        to_odd = part(halves, -j) + from_even.astype(F32)
        to_even = part(halves, j) + from_odd.astype(F32)
    from_odd = col_swap(to_odd.astype(BF16), True)
    from_even = col_swap(to_even.astype(BF16), False)
    total = part(halves, 0) + from_even.astype(F32) + from_odd.astype(F32)

    total, all_inputs, all_grads = lax.optimization_barrier((total, all_inputs, all_grads))
    hidden_mine, slope = gelu_and_slope(total[:, 0] + bias_in)
    both = jnp.stack([hidden_mine.astype(BF16), (total[:, 1] * slope).astype(BF16)], axis=1)

    everything = jnp.zeros((2, 2, 8, 32, hidden_here), BF16)
    evens, odds = [both], [both]
    for _ in range(3):
        from_even, from_odd = col_swap(odds[-1], False), col_swap(evens[-1], True)
        evens.append(from_even)
        odds.append(from_odd)
    opposite = jnp.concatenate([col_swap(odds[3][:1], False), col_swap(evens[3][1:], True)])
    for j, block in enumerate(evens + [opposite] + odds[:0:-1]):
        everything = lax.dynamic_update_slice_in_dim(everything, block[:, :, None], (me + way * j) % 8, 2)
    everything = everything.reshape(2, 2, HALF, hidden_here)

    came_out = swap_cores(matmul(everything[1, 0], w_out).astype(BF16))
    came_grad = swap_cores(contract_cols(everything[1, 1], w_in).astype(BF16))
    kept_out = matmul(everything[0, 0], w_out) + came_out.astype(F32)
    kept_grad = contract_cols(everything[0, 1], w_in) + came_grad.astype(F32)
    kept = [
        jnp.stack([x.reshape(4, 4, 16, features)[k] for x in (kept_out, kept_grad)]) for k in range(4)
    ]
    sent = [x.astype(BF16) for x in kept[1:]]
    everything, all_inputs, all_grads, *sent = lax.optimization_barrier((everything, all_inputs, all_grads, *sent))
    came = {k: plane_swap(sent[k - 1], k, False) for k in (2, 1, 3)}
    plane_sum = kept[0]
    for k in (1, 2, 3):
        plane_sum = plane_sum + came[k].astype(F32)
    came = {k: plane_swap(plane_sum[:, k].astype(BF16), k, True) for k in (2, 1, 3)}
    line_sum = plane_sum[:, 0]
    for k in (1, 2, 3):
        line_sum = line_sum + came[k].astype(F32)
    result = line_sum.astype(BF16)

    hidden = everything[:, 0].reshape(TOKENS, hidden_here)
    pre_grad = everything[:, 1].reshape(TOKENS, hidden_here)
    bias_grad = jnp.sum(pre_grad.astype(F32), axis=0) * grad_scale
    w_out_grad = (contract_rows(hidden, all_grads) * grad_scale).astype(BF16)
    w_in_grad = (contract_rows(all_inputs, pre_grad) * grad_scale).astype(BF16)
    return (result[0], result[1], w_in_grad, w_out_grad, bias_grad)


def solution(mesh):
    placed = (P("row", "col"), P("col", "row"), P("row"), P("row", "col"), P("row", "col"))
    return jax.shard_map(
        local,
        mesh=mesh,
        in_specs=placed,
        out_specs=(P("row", "col"), P("row", "col"), P("col", "row"), P("row", "col"), P("row")),
        check_vma=False,
    )
```

```python
import math

import jax
import jax.numpy as jnp
from jax import lax
from jax.sharding import PartitionSpec as P

TOKENS = 512
HALF = 256
BF16 = jnp.bfloat16
F32 = jnp.float32

root_coef = math.sqrt(2.0 / math.pi)


def gelu_and_slope(values):
    inner = root_coef * (values + 0.044715 * values * values * values)
    tanh_val = jnp.tanh(inner)
    gelu = 0.5 * values * (1.0 + tanh_val)
    slope = 0.5 * (1.0 + tanh_val) + 0.5 * values * (1.0 - tanh_val * tanh_val) * root_coef * (
        1.0 + 3.0 * 0.044715 * values * values
    )
    return gelu, slope


def matmul(left, right):
    return jnp.dot(left, right, preferred_element_type=F32)


def contract_rows(left, right):
    return lax.dot_general(
        left, right, (((0,), (0,)), ((), ())), preferred_element_type=F32
    )


def contract_cols(left, right):
    return lax.dot_general(
        left, right, (((1,), (1,)), ((), ())), preferred_element_type=F32
    )


def row_of(y, x, core):
    return (y * 4 + x) * 2 + core


def ring_partner(at, size, odd_links):
    return (at + 1) % size if (at % 2 == 1) == odd_links else (at - 1) % size


def plane_swap(values, kind, first):
    pairs = []
    for y in range(4):
        for x in range(4):
            for core in range(2):
                along_x = (core == 0) == first
                at = x if along_x else y
                to = (at + 2) % 4 if kind == 2 else ring_partner(at, 4, kind == 3)
                pairs.append((row_of(y, x, core), row_of(y, to, core) if along_x else row_of(to, x, core)))
    return lax.ppermute(values, "row", pairs)


def swap_cores(values):
    return lax.ppermute(values, "row", [(i, i ^ 1) for i in range(32)])


def col_swap(values, odd_links):
    return lax.ppermute(values, "col", [(i, ring_partner(i, 8, odd_links)) for i in range(8)])


def local(activations, w_in, bias_in, w_out, cotangent):
    grad_scale = jnp.float32(1.0 / math.sqrt(TOKENS))
    features = activations.shape[1]
    hidden_here = w_in.shape[1]
    me = lax.axis_index("col")
    way = 1 - 2 * (me % 2)

    mine = jnp.stack([activations, cotangent])
    got = {k: plane_swap(mine, k, True) for k in (2, 1, 3)}
    line = lax.optimization_barrier(jnp.stack([mine, got[1], got[2], got[3]], axis=1))
    got = {k: plane_swap(line, k, False) for k in (2, 1, 3)}
    own = jnp.zeros((2, 4, 4, 16, features), BF16)
    for k, piece in ((0, line), (2, got[2]), (1, got[1]), (3, got[3])):
        own = lax.dynamic_update_slice_in_dim(own, piece[:, None], k, 1)
    own = own.reshape(2, HALF, features)
    other = swap_cores(own)

    def first_products(tokens):
        pre = matmul(tokens[0], w_in)
        pre, grads = lax.optimization_barrier((pre, tokens[1]))
        return pre, contract_cols(grads, w_out)

    own_parts = first_products(own)

    def part(halves, j):
        at = ((me + way * j) % 8) * 32
        return jnp.stack(
            [jnp.stack([lax.dynamic_slice_in_dim(x, at, 32, 0) for x in half]) for half in halves]
        )

    far_own = part([own_parts], 4).astype(BF16)
    far_own, other = lax.optimization_barrier((far_own, other))
    from_even = col_swap(far_own, False)
    other_parts = first_products(other)
    from_odd = col_swap(part([other_parts], 4).astype(BF16), True)
    halves = [own_parts, other_parts]
    from_even, own, other = lax.optimization_barrier((from_even, own, other))
    all_inputs = jnp.concatenate([own[0], other[0]])
    all_grads = jnp.concatenate([own[1], other[1]])
    to_odd = jnp.concatenate([part([own_parts], -3) + from_even.astype(F32), part([other_parts], -3)])
    to_even = jnp.concatenate([part([own_parts], 3), part([other_parts], 3) + from_odd.astype(F32)])
    for j in (2, 1):
        from_odd = col_swap(to_odd.astype(BF16), True)
        from_even = col_swap(to_even.astype(BF16), False)
        to_odd = part(halves, -j) + from_even.astype(F32)
        to_even = part(halves, j) + from_odd.astype(F32)
    from_odd = col_swap(to_odd.astype(BF16), True)
    from_even = col_swap(to_even.astype(BF16), False)
    total = part(halves, 0) + from_even.astype(F32) + from_odd.astype(F32)

    total, all_inputs, all_grads = lax.optimization_barrier((total, all_inputs, all_grads))
    hidden_mine, slope = gelu_and_slope(total[:, 0] + bias_in)
    both = jnp.stack([hidden_mine.astype(BF16), (total[:, 1] * slope).astype(BF16)], axis=1)

    everything = jnp.zeros((2, 2, 8, 32, hidden_here), BF16)
    evens, odds = [both], [both]
    for _ in range(3):
        from_even, from_odd = col_swap(odds[-1], False), col_swap(evens[-1], True)
        evens.append(from_even)
        odds.append(from_odd)
    opposite = jnp.concatenate([col_swap(odds[3][:1], False), col_swap(evens[3][1:], True)])
    for j, block in enumerate(evens + [opposite] + odds[:0:-1]):
        everything = lax.dynamic_update_slice_in_dim(everything, block[:, :, None], (me + way * j) % 8, 2)
    everything = everything.reshape(2, 2, HALF, hidden_here)

    came_out = swap_cores(matmul(everything[1, 0], w_out).astype(BF16))
    came_grad = swap_cores(contract_cols(everything[1, 1], w_in).astype(BF16))
    kept_out = matmul(everything[0, 0], w_out) + came_out.astype(F32)
    kept_grad = contract_cols(everything[0, 1], w_in) + came_grad.astype(F32)
    kept = [
        jnp.stack([x.reshape(4, 4, 16, features)[k] for x in (kept_out, kept_grad)]) for k in range(4)
    ]
    sent = [x.astype(BF16) for x in kept[1:]]
    everything, all_inputs, all_grads, *sent = lax.optimization_barrier((everything, all_inputs, all_grads, *sent))
    came = {k: plane_swap(sent[k - 1], k, False) for k in (2, 1, 3)}
    plane_sum = kept[0]
    for k in (1, 2, 3):
        plane_sum = plane_sum + came[k].astype(F32)
    came = {k: plane_swap(plane_sum[:, k].astype(BF16), k, True) for k in (2, 1, 3)}
    line_sum = plane_sum[:, 0]
    for k in (1, 2, 3):
        line_sum = line_sum + came[k].astype(F32)
    result = line_sum.astype(BF16)

    hidden = everything[:, 0].reshape(TOKENS, hidden_here)
    pre_grad = everything[:, 1].reshape(TOKENS, hidden_here)
    bias_grad = jnp.sum(pre_grad.astype(F32), axis=0) * grad_scale
    w_out_grad = (contract_rows(hidden, all_grads) * grad_scale).astype(BF16)
    w_in_grad = (contract_rows(all_inputs, pre_grad) * grad_scale).astype(BF16)
    return (result[0], result[1], w_in_grad, w_out_grad, bias_grad)


def solution(mesh):
    placed = (P("row", "col"), P("col", "row"), P("row"), P("row", "col"), P("row", "col"))
    return jax.shard_map(
        local,
        mesh=mesh,
        in_specs=placed,
        out_specs=(P("row", "col"), P("row", "col"), P("col", "row"), P("row", "col"), P("row")),
        check_vma=False,
    )
```

```python
import math

import jax
import jax.numpy as jnp
from jax import lax
from jax.sharding import PartitionSpec as P

TOKENS = 512
HALF = 256
BF16 = jnp.bfloat16
F32 = jnp.float32

root_coef = math.sqrt(2.0 / math.pi)


def gelu_and_slope(values):
    inner = root_coef * (values + 0.044715 * values * values * values)
    tanh_val = jnp.tanh(inner)
    gelu = 0.5 * values * (1.0 + tanh_val)
    slope = 0.5 * (1.0 + tanh_val) + 0.5 * values * (1.0 - tanh_val * tanh_val) * root_coef * (
        1.0 + 3.0 * 0.044715 * values * values
    )
    return gelu, slope


def matmul(left, right):
    return jnp.dot(left, right, preferred_element_type=F32)


def contract_rows(left, right):
    return lax.dot_general(
        left, right, (((0,), (0,)), ((), ())), preferred_element_type=F32
    )


def contract_cols(left, right):
    return lax.dot_general(
        left, right, (((1,), (1,)), ((), ())), preferred_element_type=F32
    )


def row_of(y, x, core):
    return (y * 4 + x) * 2 + core


def ring_partner(at, size, odd_links):
    return (at + 1) % size if (at % 2 == 1) == odd_links else (at - 1) % size


def plane_swap(values, kind, first):
    pairs = []
    for y in range(4):
        for x in range(4):
            for core in range(2):
                along_x = (core == 0) == first
                at = x if along_x else y
                to = (at + 2) % 4 if kind == 2 else ring_partner(at, 4, kind == 3)
                pairs.append((row_of(y, x, core), row_of(y, to, core) if along_x else row_of(to, x, core)))
    return lax.ppermute(values, "row", pairs)


def swap_cores(values):
    return lax.ppermute(values, "row", [(i, i ^ 1) for i in range(32)])


def col_swap(values, odd_links):
    return lax.ppermute(values, "col", [(i, ring_partner(i, 8, odd_links)) for i in range(8)])


def local(activations, w_in, bias_in, w_out, cotangent):
    grad_scale = jnp.float32(1.0 / math.sqrt(TOKENS))
    features = activations.shape[1]
    hidden_here = w_in.shape[1]
    me = lax.axis_index("col")
    way = 1 - 2 * (me % 2)

    mine = jnp.stack([activations, cotangent])
    got = {k: plane_swap(mine, k, True) for k in (2, 1, 3)}
    line = lax.optimization_barrier(jnp.stack([mine, got[1], got[2], got[3]], axis=1))
    got = {k: plane_swap(line, k, False) for k in (2, 1, 3)}
    own = jnp.zeros((2, 4, 4, 16, features), BF16)
    for k, piece in ((0, line), (2, got[2]), (1, got[1]), (3, got[3])):
        own = lax.dynamic_update_slice_in_dim(own, piece[:, None], k, 1)
    own = own.reshape(2, HALF, features)
    other = [swap_cores(own[0]), swap_cores(own[1])]

    own_pre = matmul(own[0], w_in)
    other_pre = matmul(other[0], w_in)
    other_pre, grads = lax.optimization_barrier((other_pre, own[1]))
    own_parts = own_pre, contract_cols(grads, w_out)

    def part(halves, j):
        at = ((me + way * j) % 8) * 32
        return jnp.stack(
            [jnp.stack([lax.dynamic_slice_in_dim(x, at, 32, 0) for x in half]) for half in halves]
        )

    far_own = part([own_parts], 4).astype(BF16)
    far_own, other[1] = lax.optimization_barrier((far_own, other[1]))
    from_even = col_swap(far_own, False)
    other_parts = other_pre, contract_cols(other[1], w_out)
    from_odd = col_swap(part([other_parts], 4).astype(BF16), True)
    halves = [own_parts, other_parts]
    from_even, own, other = lax.optimization_barrier((from_even, own, other))
    all_inputs = jnp.concatenate([own[0], other[0]])
    all_grads = jnp.concatenate([own[1], other[1]])
    to_odd = jnp.concatenate([part([own_parts], -3) + from_even.astype(F32), part([other_parts], -3)])
    to_even = jnp.concatenate([part([own_parts], 3), part([other_parts], 3) + from_odd.astype(F32)])
    for j in (2, 1):
        from_odd = col_swap(to_odd.astype(BF16), True)
        from_even = col_swap(to_even.astype(BF16), False)
        to_odd = part(halves, -j) + from_even.astype(F32)
        to_even = part(halves, j) + from_odd.astype(F32)
    from_odd = col_swap(to_odd.astype(BF16), True)
    from_even = col_swap(to_even.astype(BF16), False)
    total = part(halves, 0) + from_even.astype(F32) + from_odd.astype(F32)

    total, all_inputs, all_grads = lax.optimization_barrier((total, all_inputs, all_grads))
    hidden_mine, slope = gelu_and_slope(total[:, 0] + bias_in)
    both = jnp.stack([hidden_mine.astype(BF16), (total[:, 1] * slope).astype(BF16)], axis=1)

    everything = jnp.zeros((2, 2, 8, 32, hidden_here), BF16)
    evens, odds = [both], [both]
    for _ in range(3):
        from_even, from_odd = col_swap(odds[-1], False), col_swap(evens[-1], True)
        evens.append(from_even)
        odds.append(from_odd)
    opposite = jnp.concatenate([col_swap(odds[3][:1], False), col_swap(evens[3][1:], True)])
    for j, block in enumerate(evens + [opposite] + odds[:0:-1]):
        everything = lax.dynamic_update_slice_in_dim(everything, block[:, :, None], (me + way * j) % 8, 2)
    everything = everything.reshape(2, 2, HALF, hidden_here)

    came_out = swap_cores(matmul(everything[1, 0], w_out).astype(BF16))
    came_grad = swap_cores(contract_cols(everything[1, 1], w_in).astype(BF16))
    kept_out = matmul(everything[0, 0], w_out) + came_out.astype(F32)
    kept_grad = contract_cols(everything[0, 1], w_in) + came_grad.astype(F32)
    kept = [
        jnp.stack([x.reshape(4, 4, 16, features)[k] for x in (kept_out, kept_grad)]) for k in range(4)
    ]
    sent = [x.astype(BF16) for x in kept[1:]]
    everything, all_inputs, all_grads, *sent = lax.optimization_barrier((everything, all_inputs, all_grads, *sent))
    came = {k: plane_swap(sent[k - 1], k, False) for k in (2, 1, 3)}
    plane_sum = kept[0]
    for k in (1, 2, 3):
        plane_sum = plane_sum + came[k].astype(F32)
    came = {k: plane_swap(plane_sum[:, k].astype(BF16), k, True) for k in (2, 1, 3)}
    line_sum = plane_sum[:, 0]
    for k in (1, 2, 3):
        line_sum = line_sum + came[k].astype(F32)
    result = line_sum.astype(BF16)

    hidden = everything[:, 0].reshape(TOKENS, hidden_here)
    pre_grad = everything[:, 1].reshape(TOKENS, hidden_here)
    bias_grad = jnp.sum(pre_grad.astype(F32), axis=0) * grad_scale
    w_out_grad = (contract_rows(hidden, all_grads) * grad_scale).astype(BF16)
    w_in_grad = (contract_rows(all_inputs, pre_grad) * grad_scale).astype(BF16)
    return (result[0], result[1], w_in_grad, w_out_grad, bias_grad)


def solution(mesh):
    placed = (P("row", "col"), P("col", "row"), P("row"), P("row", "col"), P("row", "col"))
    return jax.shard_map(
        local,
        mesh=mesh,
        in_specs=placed,
        out_specs=(P("row", "col"), P("row", "col"), P("col", "row"), P("row", "col"), P("row")),
        check_vma=False,
    )
```

```python
import math

import jax
import jax.numpy as jnp
from jax import lax
from jax.sharding import PartitionSpec as P

TOKENS = 512
HALF = 256
BF16 = jnp.bfloat16
F32 = jnp.float32

root_coef = math.sqrt(2.0 / math.pi)


def gelu_and_slope(values):
    inner = root_coef * (values + 0.044715 * values * values * values)
    tanh_val = jnp.tanh(inner)
    gelu = 0.5 * values * (1.0 + tanh_val)
    slope = 0.5 * (1.0 + tanh_val) + 0.5 * values * (1.0 - tanh_val * tanh_val) * root_coef * (
        1.0 + 3.0 * 0.044715 * values * values
    )
    return gelu, slope


def matmul(left, right):
    return jnp.dot(left, right, preferred_element_type=F32)


def contract_rows(left, right):
    return lax.dot_general(
        left, right, (((0,), (0,)), ((), ())), preferred_element_type=F32
    )


def contract_cols(left, right):
    return lax.dot_general(
        left, right, (((1,), (1,)), ((), ())), preferred_element_type=F32
    )


def row_of(y, x, core):
    return (y * 4 + x) * 2 + core


def ring_partner(at, size, odd_links):
    return (at + 1) % size if (at % 2 == 1) == odd_links else (at - 1) % size


def plane_swap(values, kind, first):
    pairs = []
    for y in range(4):
        for x in range(4):
            for core in range(2):
                along_x = (core == 0) == first
                at = x if along_x else y
                to = (at + 2) % 4 if kind == 2 else ring_partner(at, 4, kind == 3)
                pairs.append((row_of(y, x, core), row_of(y, to, core) if along_x else row_of(to, x, core)))
    return lax.ppermute(values, "row", pairs)


def swap_cores(values):
    return lax.ppermute(values, "row", [(i, i ^ 1) for i in range(32)])


def col_swap(values, odd_links):
    return lax.ppermute(values, "col", [(i, ring_partner(i, 8, odd_links)) for i in range(8)])


def local(activations, w_in, bias_in, w_out, cotangent):
    grad_scale = jnp.float32(1.0 / math.sqrt(TOKENS))
    features = activations.shape[1]
    hidden_here = w_in.shape[1]
    me = lax.axis_index("col")
    way = 1 - 2 * (me % 2)

    mine = jnp.stack([activations, cotangent])
    got = {k: plane_swap(mine, k, True) for k in (2, 1, 3)}
    line = lax.optimization_barrier(jnp.stack([mine, got[1], got[2], got[3]], axis=1))
    got = {k: plane_swap(line, k, False) for k in (2, 1, 3)}
    own = []
    for which in range(2):
        held = jnp.zeros((4, 4, 16, features), BF16)
        for k, piece in ((0, line), (2, got[2]), (1, got[1]), (3, got[3])):
            held = lax.dynamic_update_slice_in_dim(held, piece[which][None], k, 0)
        own.append(held.reshape(HALF, features))
    other = [swap_cores(own[0]), swap_cores(own[1])]

    own_pre = matmul(own[0], w_in)
    other_pre = matmul(other[0], w_in)
    other_pre, grads = lax.optimization_barrier((other_pre, own[1]))
    own_parts = own_pre, contract_cols(grads, w_out)

    def part(halves, j):
        at = ((me + way * j) % 8) * 32
        return jnp.stack(
            [jnp.stack([lax.dynamic_slice_in_dim(x, at, 32, 0) for x in half]) for half in halves]
        )

    far_own = part([own_parts], 4).astype(BF16)
    far_own, other[1] = lax.optimization_barrier((far_own, other[1]))
    from_even = col_swap(far_own, False)
    other_parts = other_pre, contract_cols(other[1], w_out)
    from_odd = col_swap(part([other_parts], 4).astype(BF16), True)
    halves = [own_parts, other_parts]
    from_even, own, other = lax.optimization_barrier((from_even, own, other))
    all_inputs = jnp.concatenate([own[0], other[0]])
    all_grads = jnp.concatenate([own[1], other[1]])
    to_odd = jnp.concatenate([part([own_parts], -3) + from_even.astype(F32), part([other_parts], -3)])
    to_even = jnp.concatenate([part([own_parts], 3), part([other_parts], 3) + from_odd.astype(F32)])
    for j in (2, 1):
        from_odd = col_swap(to_odd.astype(BF16), True)
        from_even = col_swap(to_even.astype(BF16), False)
        to_odd = part(halves, -j) + from_even.astype(F32)
        to_even = part(halves, j) + from_odd.astype(F32)
    from_odd = col_swap(to_odd.astype(BF16), True)
    from_even = col_swap(to_even.astype(BF16), False)
    total = part(halves, 0) + from_even.astype(F32) + from_odd.astype(F32)

    total, all_inputs, all_grads = lax.optimization_barrier((total, all_inputs, all_grads))
    hidden_mine, slope = gelu_and_slope(total[:, 0] + bias_in)
    both = jnp.stack([hidden_mine.astype(BF16), (total[:, 1] * slope).astype(BF16)], axis=1)

    everything = jnp.zeros((2, 2, 8, 32, hidden_here), BF16)
    evens, odds = [both], [both]
    for _ in range(3):
        from_even, from_odd = col_swap(odds[-1], False), col_swap(evens[-1], True)
        evens.append(from_even)
        odds.append(from_odd)
    opposite = jnp.concatenate([col_swap(odds[3][:1], False), col_swap(evens[3][1:], True)])
    for j, block in enumerate(evens + [opposite] + odds[:0:-1]):
        everything = lax.dynamic_update_slice_in_dim(everything, block[:, :, None], (me + way * j) % 8, 2)
    everything = everything.reshape(2, 2, HALF, hidden_here)

    came_out = swap_cores(matmul(everything[1, 0], w_out).astype(BF16))
    came_grad = swap_cores(contract_cols(everything[1, 1], w_in).astype(BF16))
    kept_out = matmul(everything[0, 0], w_out) + came_out.astype(F32)
    kept_grad = contract_cols(everything[0, 1], w_in) + came_grad.astype(F32)
    kept = [
        jnp.stack([x.reshape(4, 4, 16, features)[k] for x in (kept_out, kept_grad)]) for k in range(4)
    ]
    sent = [x.astype(BF16) for x in kept[1:]]
    everything, all_inputs, all_grads, *sent = lax.optimization_barrier((everything, all_inputs, all_grads, *sent))
    came = {k: plane_swap(sent[k - 1], k, False) for k in (2, 1, 3)}
    plane_sum = kept[0]
    for k in (1, 2, 3):
        plane_sum = plane_sum + came[k].astype(F32)
    came = {k: plane_swap(plane_sum[:, k].astype(BF16), k, True) for k in (2, 1, 3)}
    line_sum = plane_sum[:, 0]
    for k in (1, 2, 3):
        line_sum = line_sum + came[k].astype(F32)
    result = line_sum.astype(BF16)

    hidden = everything[:, 0].reshape(TOKENS, hidden_here)
    pre_grad = everything[:, 1].reshape(TOKENS, hidden_here)
    bias_grad = jnp.sum(pre_grad.astype(F32), axis=0) * grad_scale
    w_out_grad = (contract_rows(hidden, all_grads) * grad_scale).astype(BF16)
    w_in_grad = (contract_rows(all_inputs, pre_grad) * grad_scale).astype(BF16)
    return (result[0], result[1], w_in_grad, w_out_grad, bias_grad)


def solution(mesh):
    placed = (P("row", "col"), P("col", "row"), P("row"), P("row", "col"), P("row", "col"))
    return jax.shard_map(
        local,
        mesh=mesh,
        in_specs=placed,
        out_specs=(P("row", "col"), P("row", "col"), P("col", "row"), P("row", "col"), P("row")),
        check_vma=False,
    )
```

```python
import math

import jax
import jax.numpy as jnp
from jax import lax
from jax.sharding import PartitionSpec as P

TOKENS = 512
HALF = 256
BF16 = jnp.bfloat16
F32 = jnp.float32

root_coef = math.sqrt(2.0 / math.pi)


def gelu_and_slope(values):
    inner = root_coef * (values + 0.044715 * values * values * values)
    tanh_val = jnp.tanh(inner)
    gelu = 0.5 * values * (1.0 + tanh_val)
    slope = 0.5 * (1.0 + tanh_val) + 0.5 * values * (1.0 - tanh_val * tanh_val) * root_coef * (
        1.0 + 3.0 * 0.044715 * values * values
    )
    return gelu, slope


def matmul(left, right):
    return jnp.dot(left, right, preferred_element_type=F32)


def contract_rows(left, right):
    return lax.dot_general(
        left, right, (((0,), (0,)), ((), ())), preferred_element_type=F32
    )


def contract_cols(left, right):
    return lax.dot_general(
        left, right, (((1,), (1,)), ((), ())), preferred_element_type=F32
    )


def row_of(y, x, core):
    return (y * 4 + x) * 2 + core


def ring_partner(at, size, odd_links):
    return (at + 1) % size if (at % 2 == 1) == odd_links else (at - 1) % size


def plane_swap(values, kind, first):
    pairs = []
    for y in range(4):
        for x in range(4):
            for core in range(2):
                along_x = (core == 0) == first
                at = x if along_x else y
                to = (at + 2) % 4 if kind == 2 else ring_partner(at, 4, kind == 3)
                pairs.append((row_of(y, x, core), row_of(y, to, core) if along_x else row_of(to, x, core)))
    return lax.ppermute(values, "row", pairs)


def swap_cores(values):
    return lax.ppermute(values, "row", [(i, i ^ 1) for i in range(32)])


def col_swap(values, odd_links):
    return lax.ppermute(values, "col", [(i, ring_partner(i, 8, odd_links)) for i in range(8)])


def local(activations, w_in, bias_in, w_out, cotangent):
    grad_scale = jnp.float32(1.0 / math.sqrt(TOKENS))
    features = activations.shape[1]
    hidden_here = w_in.shape[1]
    me = lax.axis_index("col")
    way = 1 - 2 * (me % 2)

    mine = jnp.stack([activations, cotangent])
    got = {k: plane_swap(mine, k, True) for k in (2, 1, 3)}
    line = lax.optimization_barrier(jnp.stack([mine, got[1], got[2], got[3]], axis=1))
    got = {k: plane_swap(line, k, False) for k in (2, 1, 3)}
    own = jnp.zeros((2, 4, 4, 16, features), BF16)
    for k, piece in ((0, line), (2, got[2]), (1, got[1]), (3, got[3])):
        own = lax.dynamic_update_slice_in_dim(own, piece[:, None], k, 1)
    own = own.reshape(2, HALF, features)
    other = swap_cores(own)

    def first_products(tokens):
        pre = matmul(tokens[0], w_in)
        pre, grads = lax.optimization_barrier((pre, tokens[1]))
        return pre, contract_cols(grads, w_out)

    own_parts = first_products(own)

    def part(halves, j):
        at = ((me + way * j) % 8) * 32
        return jnp.stack(
            [jnp.stack([lax.dynamic_slice_in_dim(x, at, 32, 0) for x in half]) for half in halves]
        )

    far_own = part([own_parts], 4).astype(BF16)
    far_own, other = lax.optimization_barrier((far_own, other))
    from_even = col_swap(far_own, False)
    other_parts = first_products(other)
    from_odd = col_swap(part([other_parts], 4).astype(BF16), True)
    halves = [own_parts, other_parts]
    from_even, own, other = lax.optimization_barrier((from_even, own, other))
    all_inputs = jnp.concatenate([own[0], other[0]])
    all_grads = jnp.concatenate([own[1], other[1]])
    to_odd = jnp.concatenate([part([own_parts], -3) + from_even.astype(F32), part([other_parts], -3)])
    to_even = jnp.concatenate([part([own_parts], 3), part([other_parts], 3) + from_odd.astype(F32)])
    for j in (2, 1):
        from_odd = col_swap(to_odd.astype(BF16), True)
        from_even = col_swap(to_even.astype(BF16), False)
        to_odd = part(halves, -j) + from_even.astype(F32)
        to_even = part(halves, j) + from_odd.astype(F32)
    from_odd = col_swap(to_odd.astype(BF16), True)
    from_even = col_swap(to_even.astype(BF16), False)
    total = part(halves, 0) + from_even.astype(F32) + from_odd.astype(F32)

    total, all_inputs, all_grads = lax.optimization_barrier((total, all_inputs, all_grads))
    hidden_mine, slope = gelu_and_slope(total[:, 0] + bias_in)
    both = jnp.stack([hidden_mine.astype(BF16), (total[:, 1] * slope).astype(BF16)], axis=1)

    everything = jnp.zeros((2, 2, 8, 32, hidden_here), BF16)
    evens, odds = [both], [both]
    for _ in range(3):
        from_even, from_odd = col_swap(odds[-1], False), col_swap(evens[-1], True)
        evens.append(from_even)
        odds.append(from_odd)
    opposite = jnp.concatenate([col_swap(odds[3][:1], False), col_swap(evens[3][1:], True)])
    for j, block in enumerate(evens + [opposite] + odds[:0:-1]):
        everything = lax.dynamic_update_slice_in_dim(everything, block[:, :, None], (me + way * j) % 8, 2)
    everything = everything.reshape(2, 2, HALF, hidden_here)

    came_out = swap_cores(matmul(everything[1, 0], w_out).astype(BF16))
    came_grad = swap_cores(contract_cols(everything[1, 1], w_in).astype(BF16))
    kept_out = matmul(everything[0, 0], w_out) + came_out.astype(F32)
    kept_grad = contract_cols(everything[0, 1], w_in) + came_grad.astype(F32)
    kept = [
        jnp.stack([x.reshape(4, 4, 16, features)[k] for x in (kept_out, kept_grad)]) for k in range(4)
    ]
    sent = [x.astype(BF16) for x in kept[1:]]
    everything, all_inputs, all_grads, *sent = lax.optimization_barrier((everything, all_inputs, all_grads, *sent))
    came = {k: plane_swap(sent[k - 1], k, False) for k in (3, 1, 2)}
    plane_sum = kept[0]
    for k in (1, 2, 3):
        plane_sum = plane_sum + came[k].astype(F32)
    came = {k: plane_swap(plane_sum[:, k].astype(BF16), k, True) for k in (3, 1, 2)}
    line_sum = plane_sum[:, 0]
    for k in (1, 2, 3):
        line_sum = line_sum + came[k].astype(F32)
    result = line_sum.astype(BF16)

    hidden = everything[:, 0].reshape(TOKENS, hidden_here)
    pre_grad = everything[:, 1].reshape(TOKENS, hidden_here)
    bias_grad = jnp.sum(pre_grad.astype(F32), axis=0) * grad_scale
    w_out_grad = (contract_rows(hidden, all_grads) * grad_scale).astype(BF16)
    w_in_grad = (contract_rows(all_inputs, pre_grad) * grad_scale).astype(BF16)
    return (result[0], result[1], w_in_grad, w_out_grad, bias_grad)


def solution(mesh):
    placed = (P("row", "col"), P("col", "row"), P("row"), P("row", "col"), P("row", "col"))
    return jax.shard_map(
        local,
        mesh=mesh,
        in_specs=placed,
        out_specs=(P("row", "col"), P("row", "col"), P("col", "row"), P("row", "col"), P("row")),
        check_vma=False,
    )
```
